1024 devices in a mesh: replica: 4 (over z_lo), fsdp: 256 (over z_hi, x, y, core).
Axes of the slice: x: 4, y: 8, z: 16 (z_hi: 4, z_lo: 4; z = z_hi * 4 + z_lo), core: 2. Of those that a mesh axis runs over, the one named last changes fastest.
Arguments:
- tokens: bfloat16 [196608, 8192], P(('replica', 'fsdp')), may hold values from -6 to 6
- outer_base: float32 [8192, 256], P('fsdp'), may hold values from -5 to 5
- outer_momentum: float32 [8192, 256], P('fsdp'), may hold values from -3 to 3
- replica_weights: bfloat16 [4, 8192, 256], P('replica', 'fsdp'), may hold values from -8 to 8
- block_exponent: int32 [4, 8192, 2], P('replica', 'fsdp'), may hold values from -11 to -4
Outputs:
- key_value: bfloat16 [196608, 256], P(('replica', 'fsdp'))
- next_base: float32 [8192, 256], P('fsdp', 'replica')
- next_momentum: float32 [8192, 256], P('fsdp', 'replica')
The draws below stay inside these ranges and needn't reach their ends.
All inputs are finite; a program needn't handle non-finite values.
Results may differ from the reference program's by a relative error of at most 0.007.
Values may be sent and summed in bfloat16 or wider, within the bound.
A program may use at most 32 MiB of HBM per device.

```python
import jax
import jax.numpy as jnp
from jax import lax

D = 8192
BLOCK = 128
TOK_DEV = 192
KV = 256
TOKENS = 196608
N_REPLICA = 4


def shared_base(key):
    return jnp.clip(jax.random.normal(key, (D, KV), jnp.float32), -5.0, 5.0)


def draw_outer_base(key, part):
    return shared_base(key)


def draw_replica_weights(key, part):
    common = shared_base(key)
    key = jax.random.fold_in(key, 7)
    first_key, second_key = jax.random.split(key, 2)
    row_scale = jnp.exp(jax.random.uniform(second_key, (N_REPLICA, D, 1), jnp.float32, jnp.log(0.1), jnp.log(1.0)))
    noise = jax.random.normal(first_key, (N_REPLICA, D, KV), jnp.float32)
    drift = 0.3 * row_scale * jnp.clip(noise, -6.0, 6.0)
    return jnp.clip(common[None] + drift, -8.0, 8.0).astype(jnp.bfloat16)


def place_ends(entries, rng, least, high):
    shape = entries.shape
    index_at = [jax.random.randint(jax.random.fold_in(rng, axis), (), 0, shape[axis]) for axis in range(len(shape))]
    entries = entries.at[tuple(index_at)].set(least)
    longest = shape.index(max(shape))
    index_at[longest] = (index_at[longest] + 1) % shape[longest]
    return entries.at[tuple(index_at)].set(high)


def block_scale(stream_key, extent, pieces, low, high):
    factor_of, own = 1.0, jax.random.fold_in(stream_key, 6)
    for axis_at, shards_of in pieces:
        draws = jnp.exp(jax.random.uniform(jax.random.fold_in(own, axis_at), (shards_of,), jnp.float32, low / len(pieces), high / len(pieces)))
        factor_of = factor_of * jnp.repeat(draws, extent[axis_at] // shards_of).reshape([-1 if axis == axis_at else 1 for axis in range(len(extent))])
    return factor_of


def gaussian(stream_key, dims, width, limit, cuts=(), held_as=jnp.bfloat16):
    loudness = block_scale(stream_key, dims, cuts, -0.22, 0.18) if cuts else 1.0
    result = jax.random.normal(stream_key, dims, jnp.float32) * width * loudness
    return jnp.minimum(jnp.maximum(result, -limit), limit).astype(held_as)


def setup_inputs(seed: int = 0) -> dict:
    splits = jax.random.split(jax.random.key(seed), 6)
    tokens = gaussian(splits[0], (TOKENS, D), 1.0, 6.0, ((0, 1024),))
    outer_base = draw_outer_base(jax.random.fold_in(splits[5], 71), 0)
    outer_momentum = gaussian(splits[2], (D, KV), 0.3, 3.0, ((0, 256),), jnp.float32)
    replica_weights = draw_replica_weights(jax.random.fold_in(splits[5], 71), 0)
    block_exponent = place_ends(jax.random.randint(splits[4], (N_REPLICA, D, KV // BLOCK), -11, -3), jax.random.fold_in(splits[4], 1), -11, (-3) - 1).astype(jnp.int32)
    return {"tokens": tokens, "outer_base": outer_base, "outer_momentum": outer_momentum, "replica_weights": replica_weights, "block_exponent": block_exponent}


code_limit = 448.0
momentum_rate = 0.9
outer_rate = 0.7


def reference(tokens, outer_base, outer_momentum, replica_weights, block_exponent):
    difference = outer_base[None] - replica_weights.astype(jnp.float32)
    blocked = difference.reshape(N_REPLICA, D, KV // BLOCK, BLOCK)
    powers = block_exponent.astype(jnp.float32)[..., None]
    encoded = jnp.clip(blocked * jnp.exp2(-powers), -code_limit, code_limit).astype(jnp.bfloat16)
    encoded = lax.optimization_barrier(encoded)
    decoded = (encoded.astype(jnp.float32) * jnp.exp2(powers)).astype(jnp.bfloat16)
    summed = jnp.sum(decoded.astype(jnp.float32), axis=0).reshape(D, KV)
    average = summed / N_REPLICA
    next_momentum = momentum_rate * outer_momentum + average
    next_base = outer_base - outer_rate * (average + momentum_rate * next_momentum)
    weights = next_base.astype(jnp.bfloat16)

    def project(token_block):
        product = jnp.dot(token_block, weights, preferred_element_type=jnp.float32)
        return (product * (D ** -0.5)).astype(jnp.bfloat16)

    key_value = lax.map(project, tokens.reshape(-1, TOK_DEV, D)).reshape(TOKENS, KV)
    return key_value, next_base, next_momentum
```

```python
import functools

import jax
import jax.numpy as jnp
from jax import lax
from jax.experimental import pallas as pl
from jax.experimental.pallas import tpu as pltpu
from jax.sharding import PartitionSpec as P

MESH = pl.DeviceIdType.MESH
BLOCK = 128
CODE_LIMIT = 448.0
MOMENTUM_RATE = 0.9
OUTER_RATE = 0.7
LOW_EXP, HIGH_EXP = -11, -4

NX, NY, NH, NR = 4, 8, 4, 4


def place():
    r, f = lax.axis_index("replica"), lax.axis_index("fsdp")
    c, y = f % 2, (f // 2) % NY
    x, zh = (f // (2 * NY)) % NX, f // (2 * NY * NX)
    return x, y, zh, r, c


def kernel(
    tok_hbm, base_ref, mom_ref, rep_ref, exp_ref,
    kv_ref, nb_ref, nm_ref,
    tok, dec, part, w, acc, half_b,
    tok_sem, s0, r0, sh, rh, s1, r1, s2, r2, s3, r3, sc, rc,
):
    x, y, zh, r, c = place()

    def dev(x, y, zh, r, c):
        return (r, ((zh * NX + x) * NY + y) * 2 + c)

    def to_r(d):
        return dev(x, y, zh, (r + d) % NR, c)

    def to_h(d):
        return dev(x, y, (zh + d) % NH, r, c)

    def to_y(d):
        return dev(x, (y + d) % NY, zh, r, c)

    def to_x(d):
        return dev((x + d) % NX, y, zh, r, c)

    def to_z(d):
        z = (zh * NR + r + d + NR * NH) % (NR * NH)
        return dev(x, y, z // NR, z % NR, c)

    other = dev(x, y, zh, r, 1 - c)

    def pick(flag, a, b):
        return tuple(jnp.where(flag, i, j) for i, j in zip(a, b))

    tok_copy = pltpu.make_async_copy(tok_hbm, tok, tok_sem)
    tok_copy.start()

    bar = pltpu.get_barrier_semaphore()
    greet = [to_r(d) for d in range(1, NR)] + [to_h(d) for d in range(1, NH)]
    greet += [to_y(d) for d in range(1, NY)] + [to_x(d) for d in (1, 2, 3)]
    greet += [to_z(d) for d in (1, -1, -2)] + [other]
    for who in greet:
        pl.semaphore_signal(bar, inc=1, device_id=who, device_id_type=MESH)

    exps = exp_ref[0]
    up = jnp.zeros(exps.shape, jnp.float32)
    down = jnp.zeros(exps.shape, jnp.float32)
    for e in range(LOW_EXP, HIGH_EXP + 1):
        up = jnp.where(exps == e, 2.0**-e, up)
        down = jnp.where(exps == e, 2.0**e, down)
    for v in range(2):
        cols = slice(v * BLOCK, (v + 1) * BLOCK)
        diff = base_ref[:, cols] - rep_ref[0, :, cols].astype(jnp.float32)
        code = jnp.clip(diff * up[:, v : v + 1], -CODE_LIMIT, CODE_LIMIT)
        code = code.astype(jnp.bfloat16).astype(jnp.float32)
        dec[v] = (code * down[:, v : v + 1]).astype(jnp.bfloat16)

    pl.semaphore_wait(bar, len(greet))

    pending = []

    def send(src, dst, ss, rs, who):
        cp = pltpu.make_async_remote_copy(
            src_ref=src, dst_ref=dst, send_sem=ss, recv_sem=rs, device_id=who, device_id_type=MESH
        )
        cp.start()
        pending.append(cp)

    def arrive(dst, ss, rs):
        pltpu.make_async_remote_copy(
            src_ref=dst, dst_ref=dst, send_sem=ss, recv_sem=rs, device_id=other, device_id_type=MESH
        ).wait_recv()

    for d in range(1, NR):
        p = (r + d) % NR
        send(dec.at[p // 2], part.at[NR - d], s0.at[d], r0.at[NR - d], to_r(d))
    part[0] = dec[r // 2]
    for d in range(1, NR):
        arrive(part.at[d], s0.at[d], r0.at[d])
    total = part[0].astype(jnp.float32)
    for d in range(1, NR):
        total = total + part[d].astype(jnp.float32)
    average = total / NR
    mine = pl.ds(pl.multiple_of((r // 2) * BLOCK, BLOCK), BLOCK)
    new_mom = MOMENTUM_RATE * mom_ref[:, mine] + average
    new_base = base_ref[:, mine] - OUTER_RATE * (average + MOMENTUM_RATE * new_mom)
    odd = (r % 2) == 1
    piece = jnp.where(odd, new_base[16:], new_base[:16]).astype(jnp.bfloat16)

    def flip(h):
        return (h + c) % 2

    def st(h):
        return jnp.where(flip(h) == 0, x, r), jnp.where(flip(h) == 0, r, x)

    s_own, t_own = st(zh)
    w[zh, c, s_own, t_own, y] = piece

    def hs(d):
        return (zh + d) % NH

    for d in (2, 1, 3):
        cell = w.at[zh, c, s_own, t_own, y]
        send(cell, cell, sh.at[d], rh.at[NH - d], to_h(d))

    def run_wait(d):
        h = hs(d)
        s, t = st(h)
        arrive(w.at[h, c, s, t, y], sh.at[d], rh.at[d])

    def y_send(d):
        h = hs(d)
        s, t = st(h)
        cell = w.at[h, c, s, t, y]
        for e in (4, 3, 5, 2, 6, 1, 7):
            send(cell, cell, s1.at[d, e], r1.at[d, NY - e], to_y(e))

    def y_wait(d):
        h = hs(d)
        s, t = st(h)
        for e in range(1, NY):
            arrive(w.at[h, c, s, t, (y + e) % NY], s1.at[d, e], r1.at[d, e])

    def t_send(d):
        h = hs(d)
        s, t = st(h)
        row = w.at[h, c, s, t]
        for e in (2, 1, 3):
            who = pick(flip(h) == 0, to_z(e if e < 3 else -1), to_x(e))
            send(row, row, s2.at[h, e], r2.at[h, 4 - e], who)

    def t_wait(d):
        h = hs(d)
        s, t = st(h)
        for e in (1, 3, 2):
            arrive(w.at[h, c, s, (t + e) % 4], s2.at[h, e], r2.at[h, e])

    def core_send(h, block, i):
        send(block, block, sc.at[h, i], rc.at[h, i], other)

    def s_peer(h, e):
        return pick(flip(h) == 0, to_x(e), to_z(e if e < 3 else -1))

    def s_send(d):
        h = hs(d)
        s, t = st(h)
        block = w.at[h, c, s]
        for e in (1, 3):
            send(block, block, s3.at[h, e], r3.at[h, 4 - e], s_peer(h, e))
        core_send(h, block, 0)

    def s_forward(d):
        h = hs(d)
        s, t = st(h)
        for e, lo in ((3, 0), (1, 2)):
            block = w.at[h, c, (s + e) % 4]
            arrive(block, s3.at[h, e], r3.at[h, e])
            piece = block.at[pl.ds(lo, 2)]
            send(piece, piece, s3.at[h, 0 if e == 3 else 2], r3.at[h, 0 if e == 3 else 2], s_peer(h, 4 - e))
            core_send(h, block, e)

    def s_wait(d):
        h = hs(d)
        s, t = st(h)
        for k, lo in ((0, 0), (2, 2)):
            piece = w.at[h, c, (s + 2) % 4, pl.ds(lo, 2)]
            arrive(piece, s3.at[h, k], r3.at[h, k])
            core_send(h, piece, 2 if k == 0 else 4)

    def core_wait(d):
        h = hs(d)
        o = 1 - c
        so = jnp.where(flip(h) == 0, r, x)
        arrive(w.at[h, o, so], sc.at[h, 0], rc.at[h, 0])
        for e in (3, 1):
            arrive(w.at[h, o, (so + e) % 4], sc.at[h, e], rc.at[h, e])
        for i, lo in ((2, 0), (4, 2)):
            arrive(w.at[h, o, (so + 2) % 4, pl.ds(lo, 2)], sc.at[h, i], rc.at[h, i])

    def multiply(d, first):
        h = hs(d)
        depth = NY * 64

        def step(i, total):
            tiles = {}
            for cc in range(2):
                for p in range(NR):
                    turned = (h + cc) % 2 == 1
                    si, ti = jnp.where(turned, p, i), jnp.where(turned, i, p)
                    for yy in range(NY):
                        tiles[yy, cc, p] = w[h, cc, si, ti, yy]
            rows = [
                jnp.concatenate([tiles[yy, cc, q], tiles[yy, cc, 2 + q]], axis=1)
                for yy in range(NY) for cc in range(2) for q in range(2)
            ]
            weights = jnp.concatenate(rows, axis=0)
            at = pl.multiple_of((h * NX + i) * depth, depth)
            acc[...] += jnp.dot(tok[:, pl.ds(at, depth)], weights, preferred_element_type=jnp.float32)
            return total

        lax.fori_loop(0, NX, step, 0)

    y_send(0)
    nm_ref[...] = jnp.where(odd, new_mom[:, 64:], new_mom[:, :64])
    nb_ref[...] = jnp.where(odd, new_base[:, 64:], new_base[:, :64])
    acc[...] = jnp.zeros_like(acc)
    for d in (1, 3):
        run_wait(d)
        y_send(d)
    y_wait(0)
    t_send(0)
    run_wait(2)
    y_send(2)
    for d in (1, 3):
        y_wait(d)
        t_send(d)
    t_wait(0)
    s_send(0)
    y_wait(2)
    t_send(2)
    for d in (1, 3, 2):
        t_wait(d)
        s_send(d)
    tok_copy.wait()
    for d in (0, 1, 3, 2):
        s_forward(d)
    for d in (0, 1, 3, 2):
        s_wait(d)
        core_wait(d)
        multiply(d, d == 0)
    kv_ref[...] = (acc[...] * (NX * NY * NH * 64) ** -0.5).astype(jnp.bfloat16)
    for cp in pending:
        cp.wait_send()


def body(tokens, outer_base, outer_momentum, replica_weights, block_exponent):
    rows, depth = tokens.shape
    local, width = outer_base.shape
    dma = pltpu.SemaphoreType.DMA
    vmem = pl.BlockSpec(memory_space=pltpu.VMEM)
    return pl.pallas_call(
        kernel,
        out_shape=(
            jax.ShapeDtypeStruct((rows, width), jnp.bfloat16),
            jax.ShapeDtypeStruct((local, width // NR), jnp.float32),
            jax.ShapeDtypeStruct((local, width // NR), jnp.float32),
        ),
        in_specs=[pl.BlockSpec(memory_space=pl.ANY)] + [vmem] * 4,
        out_specs=(vmem, vmem, vmem),
        scratch_shapes=[
            pltpu.VMEM((rows, depth), jnp.bfloat16),
            pltpu.VMEM((2, local, BLOCK), jnp.bfloat16),
            pltpu.VMEM((NR, local, BLOCK), jnp.bfloat16),
            pltpu.VMEM((NH, 2, 4, 4, NY, 16, BLOCK), jnp.bfloat16),
            pltpu.VMEM((rows, width), jnp.float32),
            pltpu.VMEM((local, BLOCK), jnp.float32),
            dma,
            dma((NR,)), dma((NR,)),
            dma((NH,)), dma((NH,)),
            dma((NH, NY)), dma((NH, NY)),
            dma((NH, 4)), dma((NH, 4)),
            dma((NH, 4)), dma((NH, 4)),
            dma((NH, 5)), dma((NH, 5)),
        ],
        compiler_params=pltpu.CompilerParams(
            collective_id=0, has_side_effects=True, vmem_limit_bytes=40 << 20
        ),
        cost_estimate=pl.CostEstimate(
            flops=2 * rows * depth * width, bytes_accessed=2 * rows * depth, transcendentals=0
        ),
        name="outer_step_project",
    )(tokens, outer_base, outer_momentum, replica_weights, block_exponent)


def solution(mesh):
    return jax.shard_map(
        body,
        mesh=mesh,
        in_specs=(
            P(("replica", "fsdp"), None),
            P("fsdp", None),
            P("fsdp", None),
            P("replica", "fsdp", None),
            P("replica", "fsdp", None),
        ),
        out_specs=(P(("replica", "fsdp"), None), P("fsdp", "replica"), P("fsdp", "replica")),
        check_vma=False,
    )
```

```python
import functools

import jax
import jax.numpy as jnp
from jax import lax
from jax.experimental import pallas as pl
from jax.experimental.pallas import tpu as pltpu
from jax.sharding import PartitionSpec as P

MESH = pl.DeviceIdType.MESH
BLOCK = 128
CODE_LIMIT = 448.0
MOMENTUM_RATE = 0.9
OUTER_RATE = 0.7
LOW_EXP, HIGH_EXP = -11, -4

NX, NY, NH, NR = 4, 8, 4, 4


def place():
    r, f = lax.axis_index("replica"), lax.axis_index("fsdp")
    c, y = f % 2, (f // 2) % NY
    x, zh = (f // (2 * NY)) % NX, f // (2 * NY * NX)
    return x, y, zh, r, c


def kernel(
    tok_hbm, base_hbm, mom_hbm, rep_hbm, exp_hbm,
    kv_ref, nb_ref, nm_ref,
    tok, base_ref, mom_ref, rep_ref, exp_ref, turn, dec, part, w, acc,
    in_sem, s0, r0, sh, rh, s1, r1, s3, r3, rest3, s4, r4, sc, rc, ready,
):
    x, y, zh, r, c = place()
    z = zh * NR + r
    nz = NR * NH

    def dev(x, y, zh, r, c):
        return (r, ((zh * NX + x) * NY + y) * 2 + c)

    def to_r(d):
        return dev(x, y, zh, (r + d) % NR, c)

    def to_y(d):
        return dev(x, (y + d) % NY, zh, r, c)

    def to_x(d):
        return dev((x + d) % NX, y, zh, r, c)

    def at_z(z):
        return dev(x, y, z // NR, z % NR, c)

    other = dev(x, y, zh, r, 1 - c)

    def signal(sem, who):
        pl.semaphore_signal(sem, inc=1, device_id=who, device_id_type=MESH)

    loads = [
        pltpu.make_async_copy(src, dst, in_sem.at[i])
        for i, (src, dst) in enumerate(
            ((base_hbm, base_ref), (rep_hbm, rep_ref), (exp_hbm, exp_ref), (mom_hbm, mom_ref), (tok_hbm, tok))
        )
    ]
    for load in loads:
        load.start()

    edge = (r == 0) | (r == NR - 1)
    way = jnp.where(r == 0, -1, 1)

    def target(o):
        return (z + way * o + nz) % nz

    low, high, far = (zh + NH - 1) % NH, (zh + 1) % NH, (zh + 2) % NH
    upward = r < 2
    sources = (
        (low, low * NR + NR - 1, r + 1),
        (high, high * NR, NR - r),
        (far, jnp.where(upward, far * NR + NR - 1, far * NR), jnp.where(upward, 5 + r, 8 - r)),
    )

    bar = pltpu.get_barrier_semaphore()
    inside = [to_r(d) for d in range(1, NR)] + [to_y(d) for d in range(1, NY)]
    inside += [to_x(1), to_x(-1 + NX), other]
    for who in inside:
        signal(bar, who)
    for h, src, _ in sources:
        pl.when(h > zh)(functools.partial(signal, bar, at_z(src)))
    slots = range(1, 7)
    for o in slots:
        pl.when(edge & (target(o) // NR > zh))(functools.partial(signal, bar, at_z(target(o))))

    for load in loads[:4]:
        load.wait()
    exps = exp_ref[0]
    up = jnp.zeros(exps.shape, jnp.float32)
    down = jnp.zeros(exps.shape, jnp.float32)
    for e in range(LOW_EXP, HIGH_EXP + 1):
        up = jnp.where(exps == e, 2.0**-e, up)
        down = jnp.where(exps == e, 2.0**e, down)
    local = exps.shape[1]
    turn[...] = jnp.zeros_like(turn)
    turn[0:2, :local] = up
    turn[2:4, :local] = down
    scales = turn[...].T
    up, down = scales[:local, 0:2], scales[:local, 2:4]
    for v in range(2):
        cols = slice(v * BLOCK, (v + 1) * BLOCK)
        diff = base_ref[:, cols] - rep_ref[0, :, cols].astype(jnp.float32)
        code = jnp.clip(diff * up[:, v : v + 1], -CODE_LIMIT, CODE_LIMIT)
        code = code.astype(jnp.bfloat16).astype(jnp.float32)
        dec[:, cols] = (code * down[:, v : v + 1]).astype(jnp.bfloat16)

    below = sum((edge & (target(o) // NR < zh)).astype(jnp.int32) for o in slots)
    below += sum((h < zh).astype(jnp.int32) for h, _, _ in sources)
    pl.semaphore_wait(bar, len(inside) + below)

    def copy(src, dst, ss, rs, who):
        return pltpu.make_async_remote_copy(
            src_ref=src, dst_ref=dst, send_sem=ss, recv_sem=rs, device_id=who, device_id_type=MESH
        )

    def send(ref, ss, rs, who):
        copy(ref, ref, ss, rs, who).start()

    def arrive(ref, rs):
        copy(ref, ref, in_sem.at[0], rs, other).wait_recv()

    def left(ref, ss):
        copy(ref, ref, ss, in_sem.at[0], other).wait_send()

    for d in (3, 1, 2):
        copy(dec, part.at[NR - d], s0.at[d], r0.at[NR - d], to_r(d)).start()
    for h, src, o in sources:
        pl.when(h < zh)(functools.partial(signal, ready.at[o], at_z(src)))
    total = dec[...].astype(jnp.float32)
    for d in (1, 3, 2):
        arrive(part.at[d], r0.at[d])
        total = total + part[d].astype(jnp.float32)
    average = total / NR
    new_mom = MOMENTUM_RATE * mom_ref[...] + average
    new_base = base_ref[...] - OUTER_RATE * (average + MOMENTUM_RATE * new_mom)
    own = w.at[zh, x, y, c]
    own[...] = new_base.astype(jnp.bfloat16)

    across = NH - 1 - zh
    order = (zh, zh + 1 - 2 * (zh % 2), across, across + 1 - 2 * (across % 2))

    def push(o, higher):
        run = target(o) // NR

        @pl.when(edge & ((run > zh) if higher else (run < zh)))
        def _():
            if higher:
                pl.semaphore_wait(ready.at[o], 1)
            send(own, sh.at[o], rh.at[zh], at_z(target(o)))

    def push_up():
        for o in (4, 3, 2, 1, 6, 5):
            push(o, True)

    def cell(k, dx, e):
        return w.at[order[k], (x + dx) % NX, (y + e) % NY, c]

    near = (1, 7, 2, 6, 3, 5, 4)
    from_left, from_right = (0, 7, 6, 5), (1, 2, 3, 4)

    def x_send(k, e):
        mine = cell(k, 0, e)
        for d in (1, 3):
            on = from_left if d == 1 else from_right
            sem = r3.at[k, e] if e in on else rest3.at[k, 4 - d]
            send(mine, s3.at[k], sem, to_x(d))

    def launch(k):
        if k > 0:
            arrive(cell(k, 0, 0), rh.at[order[k]])
        mine = cell(k, 0, 0)
        for e in (4, 3, 5, 2, 6, 1, 7):
            send(mine, s1.at[k], r1.at[k, NY - e], to_y(e))
        x_send(k, 0)

    def take(k, e):
        arrive(cell(k, 0, e), r1.at[k, e])
        x_send(k, e)

    def forward(k, e):
        d = 3 if e in from_left else 1
        block = cell(k, d, e)
        arrive(block, r3.at[k, e])
        send(block, s4.at[k], r4.at[k, e], to_x(4 - d))

    def core_send(k, block, i):
        send(block, sc.at[k], rc.at[k, i], other)

    def own_block(k):
        core_send(k, w.at[order[k], x, :, c], 0)

    def side_block(k, d):
        block = w.at[order[k], (x + d) % NX, :, c]
        arrive(block.at[pl.ds(0, 4)], rest3.at[k, d])
        core_send(k, block, d)

    def far_cell(k, e):
        block = cell(k, 2, e)
        arrive(block, r4.at[k, e])
        core_send(k, block, 2)

    o = 1 - c
    depth = NY * 64

    def dot(h, xx):
        at = pl.multiple_of((h * NX + xx) * depth, depth)
        weights = w[h, xx].reshape(depth, weights_width)
        acc[...] += jnp.dot(tok[:, pl.ds(at, depth)], weights, preferred_element_type=jnp.float32)

    weights_width = w.shape[-1]

    def multiply(k):
        h = order[k]
        for d in (0, 3, 1):
            arrive(w.at[h, (x + d) % NX, :, o], rc.at[k, d])

        @pl.loop(0, 3)
        def _(i):
            dot(h, (x + NX - 1 + i) % NX)

    def multiply_far(k):
        h = order[k]
        xx = (x + 2) % NX
        arrive(w.at[h, xx, :, o], rc.at[k, 2])
        dot(h, xx)

    def write_step():
        for q in range(NR):
            cols = slice(q * 64, (q + 1) * 64)

            @pl.when(r == q)
            def _():
                nm_ref[...] = new_mom[:, cols]
                nb_ref[...] = new_base[:, cols]

        acc[...] = jnp.zeros_like(acc)

    def drain(k):
        left(w.at[0, 0, pl.ds(0, 7), 0], s1.at[k])
        left(w.at[0, 0], s3.at[k])
        left(w.at[0, 0, :, 0], s4.at[k])
        left(w.at[0, :, :, 0], sc.at[k])

    forwards = (0, 1, 7, 2, 6, 3, 5, 4)

    for o_ in (4, 3, 2, 1, 6, 5):
        push(o_, False)
    launch(0)
    pl.when(zh > 0)(push_up)
    write_step()
    for e in near:
        take(0, e)
    for e in forwards:
        forward(0, e)
    pl.when(zh == 0)(push_up)
    launch(1)
    own_block(0)
    side_block(0, 3)
    side_block(0, 1)
    for e in near:
        take(1, e)
    loads[4].wait()
    for e in forwards:
        far_cell(0, e)
    multiply(0)
    launch(2)
    launch(3)
    for e in forwards:
        forward(1, e)
    own_block(1)
    side_block(1, 3)
    side_block(1, 1)
    multiply_far(0)
    for e in near:
        take(2, e)
        take(3, e)
    for e in forwards:
        far_cell(1, e)
    own_block(2)
    own_block(3)
    for e in forwards:
        forward(2, e)
        forward(3, e)
    side_block(2, 3)
    side_block(2, 1)
    side_block(3, 3)
    side_block(3, 1)
    multiply(1)
    multiply_far(1)
    drain(0)
    drain(1)
    for e in forwards:
        far_cell(2, e)
        far_cell(3, e)
    multiply(2)
    multiply(3)
    multiply_far(2)
    multiply_far(3)
    kv_ref[...] = (acc[...] * (NX * NY * NH * 64) ** -0.5).astype(jnp.bfloat16)
    for d in range(1, NR):
        left(dec, s0.at[d])
    for o_ in slots:
        pl.when(edge)(functools.partial(left, own, sh.at[o_]))
    drain(2)
    drain(3)


def finish(kv_in, nb_in, nm_in, kv_ref, nb_ref, nm_ref, sems):
    copies = [
        pltpu.make_async_copy(src, dst, sems.at[i])
        for i, (src, dst) in enumerate(((kv_in, kv_ref), (nb_in, nb_ref), (nm_in, nm_ref)))
    ]
    for copy in copies:
        copy.start()
    for copy in copies:
        copy.wait()


def body(tokens, outer_base, outer_momentum, replica_weights, block_exponent):
    rows, depth = tokens.shape
    local, width = outer_base.shape
    dma = pltpu.SemaphoreType.DMA
    vmem = pl.BlockSpec(memory_space=pltpu.VMEM)
    hbm = pl.BlockSpec(memory_space=pltpu.HBM)
    f32, bf16 = jnp.float32, jnp.bfloat16
    step = jax.ShapeDtypeStruct((local, width // NR), f32)
    exponents = jnp.swapaxes(block_exponent, 1, 2)
    operands = (tokens, outer_base, outer_momentum, replica_weights, exponents)
    operands = [pltpu.with_memory_space_constraint(a, pltpu.HBM) for a in operands]
    results = pl.pallas_call(
        kernel,
        out_shape=(jax.ShapeDtypeStruct((rows, width), bf16), step, step),
        in_specs=[hbm] * 5,
        out_specs=(vmem, vmem, vmem),
        scratch_shapes=[
            pltpu.VMEM((rows, depth), bf16),
            pltpu.VMEM((local, width), f32),
            pltpu.VMEM((local, width), f32),
            pltpu.VMEM((1, local, width), bf16),
            pltpu.VMEM(exponents.shape, jnp.int32),
            pltpu.VMEM((8, BLOCK), f32),
            pltpu.VMEM((local, width), bf16),
            pltpu.VMEM((NR, local, width), bf16),
            pltpu.VMEM((NH, NX, NY, 2, local, width), bf16),
            pltpu.VMEM((rows, width), f32),
            dma((5,)),
            dma((NR,)), dma((NR,)),
            dma((7,)), dma((NH,)),
            dma((NH,)), dma((NH, NY)),
            dma((NH,)), dma((NH, NY)), dma((NH, 4)),
            dma((NH,)), dma((NH, NY)),
            dma((NH,)), dma((NH, 4)),
            pltpu.SemaphoreType.REGULAR((7,)),
        ],
        compiler_params=pltpu.CompilerParams(
            collective_id=0, has_side_effects=True, vmem_limit_bytes=32 << 20
        ),
        cost_estimate=pl.CostEstimate(
            flops=2 * rows * depth * width, bytes_accessed=2 * rows * depth, transcendentals=0
        ),
        name="outer_step_project",
    )(*operands)
    results = [pltpu.with_memory_space_constraint(a, pltpu.VMEM) for a in results]
    return pl.pallas_call(
        finish,
        out_shape=tuple(pltpu.HBM(a.shape, a.dtype) for a in results),
        in_specs=[vmem] * 3,
        out_specs=(hbm, hbm, hbm),
        scratch_shapes=[dma((3,))],
        name="write_results",
    )(*results)


def solution(mesh):
    return jax.shard_map(
        body,
        mesh=mesh,
        in_specs=(
            P(("replica", "fsdp"), None),
            P("fsdp", None),
            P("fsdp", None),
            P("replica", "fsdp", None),
            P("replica", "fsdp", None),
        ),
        out_specs=(P(("replica", "fsdp"), None), P("fsdp", "replica"), P("fsdp", "replica")),
        check_vma=False,
    )
```

```python
import functools

import jax
import jax.numpy as jnp
from jax import lax
from jax.experimental import pallas as pl
from jax.experimental.pallas import tpu as pltpu
from jax.sharding import PartitionSpec as P

MESH = pl.DeviceIdType.MESH
BLOCK = 128
CODE_LIMIT = 448.0
MOMENTUM_RATE = 0.9
OUTER_RATE = 0.7
LOW_EXP, HIGH_EXP = -11, -4

NX, NY, NH, NR = 4, 8, 4, 4


def place():
    r, f = lax.axis_index("replica"), lax.axis_index("fsdp")
    c, y = lax.rem(f, 2), lax.rem(lax.div(f, 2), NY)
    x, zh = lax.rem(lax.div(f, 2 * NY), NX), lax.div(f, 2 * NY * NX)
    return x, y, zh, r, c


def wrap(i, n):
    return jnp.where(i >= n, i - n, i)


def kernel(
    tok_hbm, base_hbm, mom_hbm, rep_hbm, exp_hbm,
    kv_ref, nb_ref, nm_ref,
    tok, base_ref, mom_ref, rep_ref, exp_ref, turn, dec, part, w, acc,
    in_sem, s0, r0, sh, rh, s1, r1, s3, r3, s4, r4, sc, rc, ready,
):
    x, y, zh, r, c = place()
    z = zh * NR + r
    nz = NR * NH

    def dev(x, y, zh, r, c):
        return (r, ((zh * NX + x) * NY + y) * 2 + c)

    def to_r(d):
        return dev(x, y, zh, wrap(r + d, NR), c)

    def to_y(d):
        return dev(x, wrap(y + d, NY), zh, r, c)

    def to_x(d):
        return dev(wrap(x + d, NX), y, zh, r, c)

    def at_z(z):
        return dev(x, y, lax.div(z, NR), lax.rem(z, NR), c)

    other = dev(x, y, zh, r, 1 - c)

    def signal(sem, who):
        pl.semaphore_signal(sem, inc=1, device_id=who, device_id_type=MESH)

    loads = [
        pltpu.make_async_copy(src, dst, in_sem.at[i])
        for i, (src, dst) in enumerate(
            ((base_hbm, base_ref), (rep_hbm, rep_ref), (exp_hbm, exp_ref), (mom_hbm, mom_ref), (tok_hbm, tok))
        )
    ]
    for load in loads:
        load.start()

    edge = (r == 0) | (r == NR - 1)
    way = jnp.where(r == 0, -1, 1)

    def target(o):
        return lax.rem(z + way * o + nz, nz)

    low, high, far = wrap(zh + NH - 1, NH), wrap(zh + 1, NH), wrap(zh + 2, NH)
    upward = r < 2
    sources = (
        (low, low * NR + NR - 1, r + 1),
        (high, high * NR, NR - r),
        (far, jnp.where(upward, far * NR + NR - 1, far * NR), jnp.where(upward, 5 + r, 8 - r)),
    )

    bar = pltpu.get_barrier_semaphore()
    inside = [to_r(d) for d in range(1, NR)] + [to_y(d) for d in range(1, NY)]
    inside += [to_x(1), to_x(-1 + NX), other]
    for who in inside:
        signal(bar, who)
    for h, src, _ in sources:
        pl.when(h > zh)(functools.partial(signal, bar, at_z(src)))
    slots = range(1, 7)
    for o in slots:
        pl.when(edge & (lax.div(target(o), NR) > zh))(functools.partial(signal, bar, at_z(target(o))))

    for load in loads[:4]:
        load.wait()
    exps = exp_ref[0]
    up = jnp.zeros(exps.shape, jnp.float32)
    down = jnp.zeros(exps.shape, jnp.float32)
    for e in range(LOW_EXP, HIGH_EXP + 1):
        up = jnp.where(exps == e, 2.0**-e, up)
        down = jnp.where(exps == e, 2.0**e, down)
    local = exps.shape[1]
    turn[...] = jnp.zeros_like(turn)
    turn[0:2, :local] = up
    turn[2:4, :local] = down
    scales = turn[...].T
    up, down = scales[:local, 0:2], scales[:local, 2:4]
    for v in range(2):
        cols = slice(v * BLOCK, (v + 1) * BLOCK)
        diff = base_ref[:, cols] - rep_ref[0, :, cols].astype(jnp.float32)
        code = jnp.clip(diff * up[:, v : v + 1], -CODE_LIMIT, CODE_LIMIT)
        code = code.astype(jnp.bfloat16).astype(jnp.float32)
        dec[:, cols] = (code * down[:, v : v + 1]).astype(jnp.bfloat16)

    below = sum((edge & (lax.div(target(o), NR) < zh)).astype(jnp.int32) for o in slots)
    below += sum((h < zh).astype(jnp.int32) for h, _, _ in sources)
    pl.semaphore_wait(bar, len(inside) + below)

    def copy(src, dst, ss, rs, who):
        return pltpu.make_async_remote_copy(
            src_ref=src, dst_ref=dst, send_sem=ss, recv_sem=rs, device_id=who, device_id_type=MESH
        )

    def send(ref, ss, rs, who):
        copy(ref, ref, ss, rs, who).start()

    def arrive(ref, rs):
        copy(ref, ref, in_sem.at[0], rs, other).wait_recv()

    def left(ref, ss):
        copy(ref, ref, ss, in_sem.at[0], other).wait_send()

    for d in (3, 1, 2):
        copy(dec, part.at[NR - d], s0.at[d], r0.at[NR - d], to_r(d)).start()
    for h, src, o in sources:
        pl.when(h < zh)(functools.partial(signal, ready.at[o], at_z(src)))
    total = dec[...].astype(jnp.float32)
    for d in (1, 3, 2):
        arrive(part.at[d], r0.at[d])
        total = total + part[d].astype(jnp.float32)
    average = total / NR
    new_mom = MOMENTUM_RATE * mom_ref[...] + average
    new_base = base_ref[...] - OUTER_RATE * (average + MOMENTUM_RATE * new_mom)
    own = w.at[c, zh, x, y]
    own[...] = new_base.astype(jnp.bfloat16)

    across = NH - 1 - zh
    order = (zh, zh + 1 - 2 * lax.rem(zh, 2), across, across + 1 - 2 * lax.rem(across, 2))

    def push(o, higher):
        run = lax.div(target(o), NR)

        @pl.when(edge & ((run > zh) if higher else (run < zh)))
        def _():
            if higher:
                pl.semaphore_wait(ready.at[o], 1)
            send(own, sh.at[o], rh.at[zh], at_z(target(o)))

    def push_up():
        for o in (4, 3, 2, 1, 6, 5):
            push(o, True)

    pair = lax.div(y, 2)
    first = [2 * wrap(pair + j, NY // 2) for j in range(NY // 2)]
    column = [wrap(x + d, NX) for d in range(NX)]
    left_x, right_x, up_y = to_x(3), to_x(1), [to_y(e) for e in range(NY)]
    from_left = (0, 3)

    def cells(k, d, j):
        return w.at[c, order[k], column[d], pl.ds(first[j], 2)]

    def launch(k):
        mine = w.at[c, order[k], x, y]
        if k > 0:
            arrive(mine, rh.at[order[k]])
        for e in (4, 3, 5, 2, 6, 1, 7):
            there = wrap(pair + NY // 2 - lax.div(wrap(y + e, NY), 2), NY // 2)
            send(mine, s1.at[k], r1.at[k, there], up_y[e])

    def take(k, j):
        mine = cells(k, 0, j)
        arrive(mine.at[pl.ds(0, 1)] if j == 0 else mine, r1.at[k, j])
        on = j in from_left
        send(mine, s3.at[k], r3.at[k, j if on else 4], right_x)
        send(mine, s3.at[k], r3.at[k, 5 if on else j], left_x)

    def forward(k, j):
        on = j in from_left
        block = cells(k, 3 if on else 1, j)
        arrive(block, r3.at[k, j])
        send(block, s4.at[k], r4.at[k, j], right_x if on else left_x)

    def core_send(k, block, i):
        send(block, sc.at[k], rc.at[k, i], other)

    def own_block(k):
        core_send(k, w.at[c, order[k], x], 0)

    def side_block(k, d):
        block = w.at[c, order[k], column[d]]
        arrive(block.at[pl.ds(0, 4)], r3.at[k, 4 if d == 3 else 5])
        core_send(k, block, d)

    def far_cells(k):
        for j in (0, 1, 3, 2):
            block = cells(k, 2, j)
            arrive(block, r4.at[k, j])
            core_send(k, block, 2)

    o = 1 - c
    depth, width = NY * 2 * w.shape[-2], w.shape[-1]

    def dot(h, xx):
        at = pl.multiple_of((h * NX + xx) * depth, depth)
        weights = jnp.concatenate([w[cc, h, xx, yy] for yy in range(NY) for cc in range(2)], axis=0)
        acc[...] += jnp.dot(tok[:, pl.ds(at, depth)], weights, preferred_element_type=jnp.float32)

    def multiply(k):
        h = order[k]
        for d in (0, 3, 1):
            arrive(w.at[o, h, column[d]], rc.at[k, d])

        @pl.loop(0, 3)
        def _(i):
            dot(h, lax.rem(x + NX - 1 + i, NX))

    def multiply_far(k):
        arrive(w.at[o, order[k], column[2]], rc.at[k, 2])
        dot(order[k], column[2])

    def write_step():
        for q in range(NR):
            cols = slice(q * 64, (q + 1) * 64)

            @pl.when(r == q)
            def _():
                nm_ref[...] = new_mom[:, cols]
                nb_ref[...] = new_base[:, cols]

        acc[...] = jnp.zeros_like(acc)

    def drain(k):
        left(w.at[0, 0, 0, pl.ds(0, 7)], s1.at[k])
        left(w.at[0, 0, pl.ds(0, 2)], s3.at[k])
        left(w.at[0, 0, 0], s4.at[k])
        left(w.at[0, 0], sc.at[k])

    near = (0, 1, 3, 2)
    for o_ in (4, 3, 2, 1, 6, 5):
        push(o_, False)
    launch(0)
    pl.when(zh > 0)(push_up)
    write_step()
    for j in near:
        take(0, j)
    for j in near:
        forward(0, j)
    pl.when(zh == 0)(push_up)
    launch(1)
    own_block(0)
    side_block(0, 3)
    side_block(0, 1)
    for j in near:
        take(1, j)
    loads[4].wait()
    far_cells(0)
    multiply(0)
    launch(2)
    launch(3)
    for j in near:
        forward(1, j)
    own_block(1)
    side_block(1, 3)
    side_block(1, 1)
    multiply_far(0)
    for j in near:
        take(2, j)
        take(3, j)
    far_cells(1)
    own_block(2)
    own_block(3)
    for j in near:
        forward(2, j)
        forward(3, j)
    side_block(2, 3)
    side_block(2, 1)
    side_block(3, 3)
    side_block(3, 1)
    multiply(1)
    multiply_far(1)
    drain(0)
    drain(1)
    far_cells(2)
    far_cells(3)
    multiply(2)
    multiply(3)
    multiply_far(2)
    multiply_far(3)
    kv_ref[...] = (acc[...] * (NX * NY * NH * 64) ** -0.5).astype(jnp.bfloat16)
    for d in range(1, NR):
        left(dec, s0.at[d])
    for o_ in slots:
        pl.when(edge)(functools.partial(left, own, sh.at[o_]))
    drain(2)
    drain(3)


def finish(kv_in, nb_in, nm_in, kv_ref, nb_ref, nm_ref, sems):
    copies = [
        pltpu.make_async_copy(src, dst, sems.at[i])
        for i, (src, dst) in enumerate(((kv_in, kv_ref), (nb_in, nb_ref), (nm_in, nm_ref)))
    ]
    for copy in copies:
        copy.start()
    for copy in copies:
        copy.wait()


def body(tokens, outer_base, outer_momentum, replica_weights, block_exponent):
    rows, depth = tokens.shape
    local, width = outer_base.shape
    dma = pltpu.SemaphoreType.DMA
    vmem = pl.BlockSpec(memory_space=pltpu.VMEM)
    hbm = pl.BlockSpec(memory_space=pltpu.HBM)
    f32, bf16 = jnp.float32, jnp.bfloat16
    step = jax.ShapeDtypeStruct((local, width // NR), f32)
    exponents = jnp.swapaxes(block_exponent, 1, 2)
    operands = (tokens, outer_base, outer_momentum, replica_weights, exponents)
    operands = [pltpu.with_memory_space_constraint(a, pltpu.HBM) for a in operands]
    results = pl.pallas_call(
        kernel,
        out_shape=(jax.ShapeDtypeStruct((rows, width), bf16), step, step),
        in_specs=[hbm] * 5,
        out_specs=(vmem, vmem, vmem),
        scratch_shapes=[
            pltpu.VMEM((rows, depth), bf16),
            pltpu.VMEM((local, width), f32),
            pltpu.VMEM((local, width), f32),
            pltpu.VMEM((1, local, width), bf16),
            pltpu.VMEM(exponents.shape, jnp.int32),
            pltpu.VMEM((8, BLOCK), f32),
            pltpu.VMEM((local, width), bf16),
            pltpu.VMEM((NR, local, width), bf16),
            pltpu.VMEM((2, NH, NX, NY, local, width), bf16),
            pltpu.VMEM((rows, width), f32),
            dma((5,)),
            dma((NR,)), dma((NR,)),
            dma((7,)), dma((NH,)),
            dma((NH,)), dma((NH, 4)),
            dma((NH,)), dma((NH, 6)),
            dma((NH,)), dma((NH, 4)),
            dma((NH,)), dma((NH, 4)),
            pltpu.SemaphoreType.REGULAR((7,)),
        ],
        compiler_params=pltpu.CompilerParams(
            collective_id=0, has_side_effects=True, vmem_limit_bytes=32 << 20
        ),
        cost_estimate=pl.CostEstimate(
            flops=2 * rows * depth * width, bytes_accessed=2 * rows * depth, transcendentals=0
        ),
        name="outer_step_project",
    )(*operands)
    results = [pltpu.with_memory_space_constraint(a, pltpu.VMEM) for a in results]
    return pl.pallas_call(
        finish,
        out_shape=tuple(pltpu.HBM(a.shape, a.dtype) for a in results),
        in_specs=[vmem] * 3,
        out_specs=(hbm, hbm, hbm),
        scratch_shapes=[dma((3,))],
        name="write_results",
    )(*results)


def solution(mesh):
    return jax.shard_map(
        body,
        mesh=mesh,
        in_specs=(
            P(("replica", "fsdp"), None),
            P("fsdp", None),
            P("fsdp", None),
            P("replica", "fsdp", None),
            P("replica", "fsdp", None),
        ),
        out_specs=(P(("replica", "fsdp"), None), P("fsdp", "replica"), P("fsdp", "replica")),
        check_vma=False,
    )
```
